32 devices in a mesh: dp: 8 (over y, x, core), tensor: 4 (over z).
Axes of the slice: x: 2, y: 2, z: 4, core: 2. Of those that a mesh axis runs over, the one named last changes fastest.
Arguments:
- inputs: bfloat16 [2048, 4096], P('dp', 'tensor'), may hold values from -6 to 6
- grad_out: bfloat16 [2048, 4096], P('dp', 'tensor'), may hold values from -6 to 6
- gate_pre: bfloat16 [2048, 3584], P('dp', 'tensor'), may hold values from -6 to 6
- up_pre: bfloat16 [2048, 3584], P('dp', 'tensor'), may hold values from -6 to 6
- down_weight: bfloat16 [3584, 4096], P('tensor', 'dp'), may hold values from -0.09375 to 0.09375
- warm_start: float32 [3, 4096, 32], P(None, 'tensor'), may hold values from -6 to 6
Outputs:
- left_factor: float32 [3, 3584, 32], P(None, 'tensor')
- right_factor: float32 [3, 4096, 32], P(None, 'tensor')
The draws below stay inside these ranges and needn't reach their ends.
All inputs are finite; a program needn't handle non-finite values.
Results may differ from the reference program's by a relative error of at most 0.003.
Values may be sent and summed in bfloat16 or wider, within the bound.
A program may use at most 64 MiB of HBM per device.

```python
import jax
import jax.numpy as jnp
from jax import lax

D = 4096
RANK = 32
TOK = 256
FF = 3584
TOKENS = 2048
N_DP = 8


def block_levels(key, extent, shards, low, largest):
    loudness, own = 1.0, jax.random.fold_in(key, 6)
    for position, blocks in shards:
        steps = jnp.exp(jax.random.uniform(jax.random.fold_in(own, position), (blocks,), jnp.float32, low / len(shards), largest / len(shards)))
        loudness = loudness * jnp.repeat(steps, extent[position] // blocks).reshape([-1 if axis == position else 1 for axis in range(len(extent))])
    return loudness


def centred(rng, shape, scale, bound, pieces=(), held_as=jnp.bfloat16):
    level = block_levels(rng, shape, pieces, -0.22, 0.18) if pieces else 1.0
    result = jax.random.normal(rng, shape, jnp.float32) * scale * level
    return jnp.minimum(jnp.maximum(result, -bound), bound).astype(held_as)


def setup_inputs(seed: int = 0) -> dict:
    arg_keys = jax.random.split(jax.random.key(seed), 7)
    inputs = centred(arg_keys[0], (TOKENS, D), 1.0, 6.0, ((0, 8), (1, 4)))
    grad_out = centred(arg_keys[1], (TOKENS, D), 1.0, 6.0, ((0, 8), (1, 4)))
    gate_pre = centred(arg_keys[2], (TOKENS, FF), 1.0, 6.0, ((0, 8), (1, 4)))
    up_pre = centred(arg_keys[3], (TOKENS, FF), 1.0, 6.0, ((0, 8), (1, 4)))
    down_weight = centred(arg_keys[4], (FF, D), FF ** -0.5, 0.09375, ((0, 4), (1, 8)))
    warm_start = centred(arg_keys[5], (3, D, RANK), 1.0, 6.0, ((1, 4),), jnp.float32)
    return dict(inputs=inputs, grad_out=grad_out, gate_pre=gate_pre, up_pre=up_pre, down_weight=down_weight, warm_start=warm_start)


def triangular_apply(lower_factor, block):
    return jax.scipy.linalg.solve_triangular(lower_factor, block.T, lower=True).T

def reference(inputs, grad_out, gate_pre, up_pre, down_weight, warm_start):
    f32 = jnp.float32
    bf16 = jnp.bfloat16
    high = lax.Precision.HIGHEST
    gate_f = gate_pre.astype(f32)
    up_f = up_pre.astype(f32)
    sigma = jax.nn.sigmoid(gate_f)
    hidden = (gate_f * sigma * up_f).astype(bf16)
    hidden_grad = jnp.dot(grad_out, down_weight.T, preferred_element_type=f32)
    gate_grad = (hidden_grad * up_f * sigma * (1.0 + gate_f * (1.0 - sigma))).astype(bf16)
    up_grad = (hidden_grad * gate_f * sigma).astype(bf16)
    pairs = ((gate_grad, inputs), (up_grad, inputs), (hidden, grad_out))
    lefts = []
    for index in range(3):
        left_part = pairs[index][0].astype(f32)
        right_part = pairs[index][1].astype(f32)
        projected = jnp.dot(right_part, warm_start[index], precision=high)
        lefts.append(jnp.dot(left_part.T, projected, precision=high) / TOK)
    left_raw = jnp.stack(lefts)
    gram = jnp.einsum('kfr,kfs->krs', left_raw, left_raw, precision=high)
    lower = jnp.linalg.cholesky(gram)
    left_factor = jax.vmap(triangular_apply)(lower, left_raw)
    rights = []
    for index in range(3):
        left_part = pairs[index][0].astype(f32)
        right_part = pairs[index][1].astype(f32)
        mapped = jnp.dot(left_part, left_factor[index], precision=high)
        rights.append(jnp.dot(right_part.T, mapped, precision=high) / TOK)
    right_factor = jnp.stack(rights) / N_DP
    return (left_factor, right_factor)
```

```python
import functools

import jax
import jax.numpy as jnp
from jax import lax
from jax.experimental import pallas as pl
from jax.experimental.pallas import tpu as pltpu
from jax.sharding import PartitionSpec as P

F32 = jnp.float32
BF16 = jnp.bfloat16
MESH = pl.DeviceIdType.MESH
HIGH = lax.Precision.HIGHEST
NN = (((1,), (0,)), ((), ()))
NT = (((1,), (1,)), ((), ()))


def flipped(index, mask):
    result, bit = index, 0
    while (1 << bit) <= mask:
        if mask & (1 << bit):
            result = result + (1 << bit) * (1 - 2 * (lax.div(index, 1 << bit) % 2))
        bit += 1
    return result


def exact_dot(left, right, dims):
    rows = left.shape[0]
    first = left.astype(BF16)
    rest = left - first.astype(F32)
    second = rest.astype(BF16)
    third = (rest - second.astype(F32)).astype(BF16)
    out = lax.dot_general(
        jnp.concatenate([first, second, third], axis=0), right, dims, preferred_element_type=F32
    )
    return out[:rows] + (out[rows : 2 * rows] + out[2 * rows :])


def inverse_cholesky(gram):
    count, rank, _ = gram.shape
    row_id = lax.broadcasted_iota(jnp.int32, (count, rank, rank), 1)
    col_id = lax.broadcasted_iota(jnp.int32, (count, rank, rank), 2)
    work = jnp.concatenate([(row_id == col_id).astype(F32), gram], axis=2)
    row_wide = lax.broadcasted_iota(jnp.int32, work.shape, 1)
    scale = jnp.zeros((count, rank, 1), F32)
    row_thin = lax.broadcasted_iota(jnp.int32, scale.shape, 1)
    for step in range(rank):
        row = work[:, step : step + 1, :]
        pivot = work[:, step : step + 1, rank + step : rank + step + 1]
        scale = jnp.where(row_thin == step, lax.rsqrt(pivot), scale)
        if step < rank - 1:
            column = work[:, :, rank + step : rank + step + 1]
            factor = column / pivot
            work = work - jnp.where(row_wide > step, factor * row, 0.0)
    return work[:, :, :rank] * scale


class Exchange:
    def __init__(self, axis, count, refs):
        self.axis, self.count = axis, count
        self.part, self.come, self.full, self.sems = refs
        self.me = lax.axis_index(axis)
        self.sent = []

    def store(self, row, value):
        share = self.part.shape[1]
        done = 0
        while done < value.shape[0]:
            index, offset = (row + done) // share, (row + done) % share
            size = min(share - offset, value.shape[0] - done)
            self.part[index, offset : offset + size, :] = value[done : done + size]
            done += size

    def scatter(self):
        self.copies = []
        for step in range(1, self.count):
            peer = lax.rem(self.me + step, self.count)
            copy = pltpu.make_async_remote_copy(
                src_ref=self.part.at[peer],
                dst_ref=self.come.at[step - 1],
                send_sem=self.sems.at[0, step - 1],
                recv_sem=self.sems.at[1, step - 1],
                device_id={self.axis: peer},
                device_id_type=MESH,
            )
            copy.start()
            self.copies.append(copy)

    def gather(self):
        total = self.part[self.me]
        for step in range(1, self.count):
            self.copies[step - 1].wait_recv()
            total = total + self.come[step - 1]
        self.full[self.me] = total
        self.later = []
        for step in range(1, self.count):
            peer = lax.rem(self.me + step, self.count)
            copy = pltpu.make_async_remote_copy(
                src_ref=self.full.at[self.me],
                dst_ref=self.full.at[self.me],
                send_sem=self.sems.at[2, step - 1],
                recv_sem=self.sems.at[3, step - 1],
                device_id={self.axis: peer},
                device_id_type=MESH,
            )
            copy.start()
            self.later.append(copy)

    def wait(self):
        for step in range(1, self.count):
            source = lax.rem(self.me + self.count - step, self.count)
            pltpu.make_async_remote_copy(
                src_ref=self.full.at[source],
                dst_ref=self.full.at[source],
                send_sem=self.sems.at[2, step - 1],
                recv_sem=self.sems.at[3, step - 1],
                device_id={self.axis: lax.rem(self.me + step, self.count)},
                device_id_type=MESH,
            ).wait_recv()

    def load(self, row, size):
        share = self.full.shape[1]
        pieces, done = [], 0
        while done < size:
            index, offset = (row + done) // share, (row + done) % share
            take = min(share - offset, size - done)
            pieces.append(self.full[index, offset : offset + take, :])
            done += take
        return jnp.concatenate(pieces, axis=0)

    def finish(self):
        for copy in self.copies + self.later:
            copy.wait_send()


def kernel(n_dp, n_tp, x_ref, g_ref, gate_ref, up_ref, w_ref, warm_ref, left_out, right_out,
           wbuf, wsend, wrecv, gfull, gsend, grecv, hg, gate_grad, up_grad, hidden,
           p0, p1, p2, p3, l0, l1, l2, l3, m0, m1, m2, m3, r0, r1, r2, r3,
           gram_own, gram_come, gram_sems):
    d, z = lax.axis_index("dp"), lax.axis_index("tensor")
    tokens = x_ref.shape[0]
    rank = warm_ref.shape[1]
    weight_columns = w_ref.shape[1]
    per = n_dp // n_tp
    halves = wbuf.shape[1]
    width = weight_columns // halves
    bits = n_dp.bit_length() - 1

    barrier = pltpu.get_barrier_semaphore()
    for step in range(1, n_dp):
        pl.semaphore_signal(barrier, inc=1, device_id={"dp": lax.rem(d + step, n_dp)}, device_id_type=MESH)
    for step in range(1, n_tp):
        pl.semaphore_signal(barrier, inc=1, device_id={"tensor": lax.rem(z + step, n_tp)}, device_id_type=MESH)
    for part in range(per):
        gfull[z * per + part] = g_ref[:, part * weight_columns : (part + 1) * weight_columns]
    pl.semaphore_wait(barrier, n_dp - 1 + n_tp - 1)

    def shard(index):
        return gfull.at[pl.ds(index * per, per)]

    def line_copy(way, hop):
        source = z - hop if way == 0 else z + hop
        target = z + 1 if way == 0 else z - 1
        return pltpu.make_async_remote_copy(
            src_ref=shard(source), dst_ref=shard(source),
            send_sem=gsend.at[way, hop], recv_sem=grecv.at[way, hop],
            device_id={"tensor": target}, device_id_type=MESH,
        )

    def line_sends(way, hop):
        if way == 0:
            return jnp.logical_and(z - hop >= 0, z < n_tp - 1)
        return jnp.logical_and(z + hop <= n_tp - 1, z > 0)

    def line_start(hop):
        for way in (0, 1):
            @pl.when(line_sends(way, hop))
            def _():
                line_copy(way, hop).start()

    def line_wait(hop):
        for way in (0, 1):
            source = z - 1 - hop if way == 0 else z + 1 + hop
            @pl.when(source >= 0 if way == 0 else source <= n_tp - 1)
            def _():
                pltpu.make_async_remote_copy(
                    src_ref=shard(source), dst_ref=shard(source),
                    send_sem=gsend.at[way, hop], recv_sem=grecv.at[way, hop],
                    device_id={"tensor": z - 1 if way == 0 else z + 1}, device_id_type=MESH,
                ).wait_recv()

    orders = [list(range(1, bits)) + [0], list(range(bits - 1, 0, -1)) + [0]]
    weight_copies = {}

    def weight_source(slot, half):
        if slot == 0:
            return w_ref.at[:, pl.ds(half * width, width)]
        return wbuf.at[slot, half]

    def weight_send(slot, half, first):
        for bit in orders[half][first:]:
            target = slot ^ (1 << bit)
            copy = pltpu.make_async_remote_copy(
                src_ref=weight_source(slot, half), dst_ref=wbuf.at[target, half],
                send_sem=wsend.at[target, half], recv_sem=wrecv.at[target, half],
                device_id={"dp": flipped(d, 1 << bit)}, device_id_type=MESH,
            )
            copy.start()
            weight_copies[target, half] = copy

    def weight_wave(position):
        for index in range(1 << position):
            for half in range(halves):
                order = orders[half]
                slot = 1 << order[position]
                for place in range(position):
                    if index & (1 << place):
                        slot |= 1 << order[place]
                weight_copies[slot, half].wait_recv()
                weight_send(slot, half, position + 1)

    line_start(0)
    for half in range(halves):
        weight_send(0, half, 0)

    total_p = Exchange("tensor", n_tp, (p0, p1, p2, p3))
    total_l = Exchange("dp", n_dp, (l0, l1, l2, l3))
    total_m = Exchange("tensor", n_tp, (m0, m1, m2, m3))
    total_r = Exchange("dp", n_dp, (r0, r1, r2, r3))
    rights = (x_ref, x_ref, g_ref)
    lefts = (gate_grad, up_grad, hidden)
    for k in range(3):
        total_p.store(k * rank, exact_dot(warm_ref[k], rights[k][...], NT))
    total_p.scatter()

    gate = gate_ref[...].astype(F32)
    up = up_ref[...].astype(F32)
    sigma = 1.0 / (1.0 + jnp.exp(-gate))
    hidden[...] = (gate * sigma * up).astype(BF16)

    total_p.gather()
    total_p.wait()
    for hop in range(n_tp - 2):
        line_wait(hop)
        line_start(hop + 1)
        if hop < bits - 1:
            weight_wave(hop)
    for position in range(n_tp - 2, bits - 1):
        weight_wave(position)
    line_wait(n_tp - 2)

    hg[...] = jnp.zeros_like(hg)

    def use(slot, half):
        hg[...] += lax.dot_general(
            gfull[flipped(d, slot), :, half * width : (half + 1) * width],
            weight_source(slot, half)[...], NT, preferred_element_type=F32,
        )

    for slot in range(0, n_dp, 2):
        for half in range(halves):
            use(slot, half)
    for slot in range(1, n_dp, 2):
        for half in range(halves):
            weight_copies[slot, half].wait_recv()
            use(slot, half)

    gate = gate_ref[...].astype(F32)
    up = up_ref[...].astype(F32)
    sigma = 1.0 / (1.0 + jnp.exp(-gate))
    hidden_grad = hg[...]
    gate_grad[...] = (hidden_grad * up * sigma * (1.0 + gate * (1.0 - sigma))).astype(BF16)
    up_grad[...] = (hidden_grad * gate * sigma).astype(BF16)

    for k in range(3):
        total_l.store(k * rank, exact_dot(total_p.load(k * rank, rank), lefts[k][...], NN) * (1.0 / tokens))
    total_l.scatter()
    total_l.gather()
    total_l.wait()

    for k in range(3):
        raw = total_l.load(k * rank, rank)
        total_m.store(k * rank, exact_dot(raw, lefts[k][...], NT))
        gram_own[k] = lax.dot_general(raw, raw, NT, precision=HIGH, preferred_element_type=F32)
    total_m.scatter()
    gram_copies = []
    for step in range(1, n_tp):
        copy = pltpu.make_async_remote_copy(
            src_ref=gram_own, dst_ref=gram_come.at[step - 1],
            send_sem=gram_sems.at[0, step - 1], recv_sem=gram_sems.at[1, step - 1],
            device_id={"tensor": lax.rem(z + step, n_tp)}, device_id_type=MESH,
        )
        copy.start()
        gram_copies.append(copy)
    total_m.gather()
    total_m.wait()

    for k in range(3):
        total_r.store(k * rank, exact_dot(total_m.load(k * rank, rank), rights[k][...], NN))
    total_r.scatter()

    gram = gram_own[...]
    for step in range(1, n_tp):
        gram_copies[step - 1].wait_recv()
        gram = gram + gram_come[step - 1]
    inverse = inverse_cholesky(gram)
    for k in range(3):
        left_out[k] = lax.dot_general(
            inverse[k], total_l.load(k * rank, rank), NN, precision=HIGH, preferred_element_type=F32
        )

    total_r.gather()
    total_r.wait()
    for k in range(3):
        right_out[k] = lax.dot_general(
            inverse[k], total_r.load(k * rank, rank), NN, precision=HIGH, preferred_element_type=F32
        ) * (1.0 / (tokens * n_dp))

    for exchange in (total_p, total_l, total_m, total_r):
        exchange.finish()
    for copy in gram_copies + list(weight_copies.values()):
        copy.wait_send()
    for hop in range(n_tp - 1):
        for way in (0, 1):
            @pl.when(line_sends(way, hop))
            def _():
                line_copy(way, hop).wait_send()


def exchange_scratch(count, rows, width):
    share = rows // count
    return [
        pltpu.VMEM((count, share, width), F32),
        pltpu.VMEM((count - 1, share, width), F32),
        pltpu.VMEM((count, share, width), F32),
        pltpu.SemaphoreType.DMA((4, count - 1)),
    ]


def shards(n_dp, n_tp, inputs, grad_out, gate_pre, up_pre, down_weight, warm_start):
    tokens, own = inputs.shape
    hidden_units, weight_columns = down_weight.shape
    count, _, rank = warm_start.shape
    halves = 2 if weight_columns % 256 == 0 else 1
    vmem = pl.BlockSpec(memory_space=pltpu.VMEM)
    left, right = pl.pallas_call(
        functools.partial(kernel, n_dp, n_tp),
        out_shape=(
            jax.ShapeDtypeStruct((count, rank, hidden_units), F32),
            jax.ShapeDtypeStruct((count, rank, own), F32),
        ),
        in_specs=[vmem] * 6,
        out_specs=(vmem, vmem),
        scratch_shapes=[
            pltpu.VMEM((n_dp, halves, hidden_units, weight_columns // halves), BF16),
            pltpu.SemaphoreType.DMA((n_dp, halves)),
            pltpu.SemaphoreType.DMA((n_dp, halves)),
            pltpu.VMEM((n_dp, tokens, weight_columns), BF16),
            pltpu.SemaphoreType.DMA((2, n_tp - 1)),
            pltpu.SemaphoreType.DMA((2, n_tp - 1)),
            pltpu.VMEM((tokens, hidden_units), F32),
            pltpu.VMEM((tokens, hidden_units), BF16),
            pltpu.VMEM((tokens, hidden_units), BF16),
            pltpu.VMEM((tokens, hidden_units), BF16),
            *exchange_scratch(n_tp, count * rank, tokens),
            *exchange_scratch(n_dp, count * rank, hidden_units),
            *exchange_scratch(n_tp, count * rank, tokens),
            *exchange_scratch(n_dp, count * rank, own),
            pltpu.VMEM((count, rank, rank), F32),
            pltpu.VMEM((n_tp - 1, count, rank, rank), F32),
            pltpu.SemaphoreType.DMA((2, n_tp - 1)),
        ],
        compiler_params=pltpu.CompilerParams(
            collective_id=0, has_side_effects=True, vmem_limit_bytes=48 * 1024 * 1024
        ),
        name="powersgd",
    )(inputs, grad_out, gate_pre, up_pre, down_weight, jnp.swapaxes(warm_start, 1, 2))
    return jnp.swapaxes(left, 1, 2), jnp.swapaxes(right, 1, 2)


def solution(mesh):
    placed = (
        P("dp", "tensor"),
        P("dp", "tensor"),
        P("dp", "tensor"),
        P("dp", "tensor"),
        P("tensor", "dp"),
        P(None, "tensor", None),
    )
    return jax.shard_map(
        functools.partial(shards, mesh.shape["dp"], mesh.shape["tensor"]),
        mesh=mesh,
        in_specs=placed,
        out_specs=(P(None, "tensor", None), P(None, "tensor", None)),
        check_vma=False,
    )
```

```python
import functools

import jax
import jax.numpy as jnp
from jax import lax
from jax.experimental import pallas as pl
from jax.experimental.pallas import tpu as pltpu
from jax.sharding import PartitionSpec as P

F32 = jnp.float32
BF16 = jnp.bfloat16
MESH = pl.DeviceIdType.MESH
HIGH = lax.Precision.HIGHEST
NN = (((1,), (0,)), ((), ()))
NT = (((1,), (1,)), ((), ()))


def flipped(index, mask):
    result, bit = index, 0
    while (1 << bit) <= mask:
        if mask & (1 << bit):
            result = result + (1 << bit) * (1 - 2 * (lax.div(index, 1 << bit) % 2))
        bit += 1
    return result


def exact_dot(left, right, dims):
    rows = left.shape[0]
    first = left.astype(BF16)
    rest = left - first.astype(F32)
    second = rest.astype(BF16)
    third = (rest - second.astype(F32)).astype(BF16)
    out = lax.dot_general(
        jnp.concatenate([first, second, third], axis=0), right, dims, preferred_element_type=F32
    )
    return out[:rows] + (out[rows : 2 * rows] + out[2 * rows :])


def inverse_cholesky(gram):
    count, rank, _ = gram.shape
    row_id = lax.broadcasted_iota(jnp.int32, (count, rank, rank), 1)
    col_id = lax.broadcasted_iota(jnp.int32, (count, rank, rank), 2)
    work = jnp.concatenate([(row_id == col_id).astype(F32), gram], axis=2)
    row_wide = lax.broadcasted_iota(jnp.int32, work.shape, 1)
    scale = jnp.zeros((count, rank, 1), F32)
    row_thin = lax.broadcasted_iota(jnp.int32, scale.shape, 1)
    for step in range(rank):
        row = work[:, step : step + 1, :]
        pivot = work[:, step : step + 1, rank + step : rank + step + 1]
        scale = jnp.where(row_thin == step, lax.rsqrt(pivot), scale)
        if step < rank - 1:
            column = work[:, :, rank + step : rank + step + 1]
            factor = column / pivot
            work = work - jnp.where(row_wide > step, factor * row, 0.0)
    return work[:, :, :rank] * scale


class Exchange:
    def __init__(self, axis, count, refs):
        self.axis, self.count = axis, count
        self.part, self.come, self.full, self.sems = refs
        self.me = lax.axis_index(axis)
        self.copies, self.later = [], []

    def store(self, row, value):
        share = self.part.shape[1]
        done = 0
        while done < value.shape[0]:
            index, offset = (row + done) // share, (row + done) % share
            size = min(share - offset, value.shape[0] - done)
            self.part[index, offset : offset + size, :] = value[done : done + size]
            done += size

    def scatter(self):
        for step in range(1, self.count):
            peer = lax.rem(self.me + step, self.count)
            copy = pltpu.make_async_remote_copy(
                src_ref=self.part.at[peer],
                dst_ref=self.come.at[step - 1],
                send_sem=self.sems.at[0, step - 1],
                recv_sem=self.sems.at[1, step - 1],
                device_id={self.axis: peer},
                device_id_type=MESH,
            )
            copy.start()
            self.copies.append(copy)

    def gather(self):
        total = self.part[self.me]
        for step in range(1, self.count):
            self.copies[step - 1].wait_recv()
            total = total + self.come[step - 1]
        self.full[self.me] = total
        for step in range(1, self.count):
            peer = lax.rem(self.me + step, self.count)
            copy = pltpu.make_async_remote_copy(
                src_ref=self.full.at[self.me],
                dst_ref=self.full.at[self.me],
                send_sem=self.sems.at[2, step - 1],
                recv_sem=self.sems.at[3, step - 1],
                device_id={self.axis: peer},
                device_id_type=MESH,
            )
            copy.start()
            self.later.append(copy)

    def wait(self):
        for step in range(1, self.count):
            source = lax.rem(self.me + self.count - step, self.count)
            pltpu.make_async_remote_copy(
                src_ref=self.full.at[source],
                dst_ref=self.full.at[source],
                send_sem=self.sems.at[2, step - 1],
                recv_sem=self.sems.at[3, step - 1],
                device_id={self.axis: lax.rem(self.me + step, self.count)},
                device_id_type=MESH,
            ).wait_recv()

    def load(self, row, size):
        share = self.full.shape[1]
        pieces, done = [], 0
        while done < size:
            index, offset = (row + done) // share, (row + done) % share
            take = min(share - offset, size - done)
            pieces.append(self.full[index, offset : offset + take, :])
            done += take
        return jnp.concatenate(pieces, axis=0)

    def finish(self):
        for copy in self.copies + self.later:
            copy.wait_send()


def kernel(n_dp, n_tp, x_hbm, g_hbm, gate_hbm, up_hbm, w_hbm, warm_hbm, left_out, right_out,
           x_ref, gate_ref, up_ref, warm_ref, load_sems, wbuf, wsend, wrecv, gfull, gsend, grecv, hg, gate_grad, up_grad, hidden,
           p0, p1, p2, p3, l0, l1, l2, l3, m0, m1, m2, m3, r0, r1, r2, r3,
           gram_own, gram_come, gram_sems):
    d, z = lax.axis_index("dp"), lax.axis_index("tensor")
    tokens = x_ref.shape[0]
    rank = warm_ref.shape[1]
    weight_columns = w_hbm.shape[1]
    per = n_dp // n_tp
    halves = wbuf.shape[1]
    width = weight_columns // halves
    bits = n_dp.bit_length() - 1

    barrier = pltpu.get_barrier_semaphore()
    for step in range(1, n_dp):
        pl.semaphore_signal(barrier, inc=1, device_id={"dp": lax.rem(d + step, n_dp)}, device_id_type=MESH)
    for step in range(1, n_tp):
        pl.semaphore_signal(barrier, inc=1, device_id={"tensor": lax.rem(z + step, n_tp)}, device_id_type=MESH)

    loads = []

    def load(source, target):
        copy = pltpu.make_async_copy(source, target, load_sems.at[len(loads)])
        copy.start()
        loads.append(copy)
        return copy

    load_g = [
        load(g_hbm.at[:, pl.ds(part * weight_columns, weight_columns)], gfull.at[z * per + part])
        for part in range(per)
    ]
    load_w = [
        load(w_hbm.at[:, pl.ds(half * width, width)], wbuf.at[0, half]) for half in range(halves)
    ]
    load_warm, load_x = load(warm_hbm, warm_ref), load(x_hbm, x_ref)
    load_gate, load_up = load(gate_hbm, gate_ref), load(up_hbm, up_ref)
    for copy in load_g:
        copy.wait()
    pl.semaphore_wait(barrier, n_dp - 1 + n_tp - 1)

    def shard(index):
        return gfull.at[pl.ds(index * per, per)]

    def line_copy(way, hop):
        source = z - hop if way == 0 else z + hop
        target = z + 1 if way == 0 else z - 1
        return pltpu.make_async_remote_copy(
            src_ref=shard(source), dst_ref=shard(source),
            send_sem=gsend.at[way, hop], recv_sem=grecv.at[way, hop],
            device_id={"tensor": target}, device_id_type=MESH,
        )

    def line_sends(way, hop):
        if way == 0:
            return jnp.logical_and(z - hop >= 0, z < n_tp - 1)
        return jnp.logical_and(z + hop <= n_tp - 1, z > 0)

    def line_start(hop):
        for way in (0, 1):
            @pl.when(line_sends(way, hop))
            def _():
                line_copy(way, hop).start()

    def line_wait(hop):
        for way in (0, 1):
            source = z - 1 - hop if way == 0 else z + 1 + hop
            @pl.when(source >= 0 if way == 0 else source <= n_tp - 1)
            def _():
                pltpu.make_async_remote_copy(
                    src_ref=shard(source), dst_ref=shard(source),
                    send_sem=gsend.at[way, hop], recv_sem=grecv.at[way, hop],
                    device_id={"tensor": z - 1 if way == 0 else z + 1}, device_id_type=MESH,
                ).wait_recv()

    orders = [list(range(1, bits)) + [0], list(range(bits - 1, 0, -1)) + [0]]
    weight_copies = {}

    def weight_send(slot, half, first):
        for bit in orders[half][first:]:
            target = slot ^ (1 << bit)
            copy = pltpu.make_async_remote_copy(
                src_ref=wbuf.at[slot, half], dst_ref=wbuf.at[target, half],
                send_sem=wsend.at[target, half], recv_sem=wrecv.at[target, half],
                device_id={"dp": flipped(d, 1 << bit)}, device_id_type=MESH,
            )
            copy.start()
            weight_copies[target, half] = copy

    def weight_wave(position):
        for index in range(1 << position):
            for half in range(halves):
                order = orders[half]
                slot = 1 << order[position]
                for place in range(position):
                    if index & (1 << place):
                        slot |= 1 << order[place]
                weight_copies[slot, half].wait_recv()
                weight_send(slot, half, position + 1)

    gram_copies = []

    def finish():
        for exchange in (total_p, total_l, total_m, total_r):
            exchange.finish()
        for copy in gram_copies + list(weight_copies.values()):
            copy.wait_send()
        for hop in range(n_tp - 1):
            for way in (0, 1):
                @pl.when(line_sends(way, hop))
                def _():
                    line_copy(way, hop).wait_send()

    line_start(0)
    for half in range(halves):
        load_w[half].wait()
        weight_send(0, half, 0)

    total_p = Exchange("tensor", n_tp, (p0, p1, p2, p3))
    total_l = Exchange("dp", n_dp, (l0, l1, l2, l3))
    total_m = Exchange("tensor", n_tp, (m0, m1, m2, m3))
    total_r = Exchange("dp", n_dp, (r0, r1, r2, r3))
    lefts = (gate_grad, up_grad, hidden)

    def right(k):
        if k < 2:
            return x_ref[...]
        return jnp.concatenate([gfull[z * per + part] for part in range(per)], axis=1)

    load_warm.wait()
    load_x.wait()
    for k in range(3):
        total_p.store(k * rank, exact_dot(warm_ref[k], right(k), NT))
    total_p.scatter()

    load_gate.wait()
    load_up.wait()
    gate = gate_ref[...].astype(F32)
    up = up_ref[...].astype(F32)
    sigma = 1.0 / (1.0 + jnp.exp(-gate))
    hidden[...] = (gate * sigma * up).astype(BF16)

    total_p.gather()
    total_p.wait()
    for hop in range(n_tp - 2):
        line_wait(hop)
        line_start(hop + 1)
        if hop < bits - 1:
            weight_wave(hop)
    for position in range(n_tp - 2, bits - 1):
        weight_wave(position)
    line_wait(n_tp - 2)

    hg[...] = jnp.zeros_like(hg)

    def use(slot, half):
        hg[...] += lax.dot_general(
            gfull[flipped(d, slot), :, half * width : (half + 1) * width],
            wbuf[slot, half], NT, preferred_element_type=F32,
        )

    for slot in range(0, n_dp, 2):
        for half in range(halves):
            use(slot, half)
    for slot in range(1, n_dp, 2):
        for half in range(halves):
            weight_copies[slot, half].wait_recv()
            use(slot, half)

    gate = gate_ref[...].astype(F32)
    up = up_ref[...].astype(F32)
    sigma = 1.0 / (1.0 + jnp.exp(-gate))
    hidden_grad = hg[...]
    gate_grad[...] = (hidden_grad * up * sigma * (1.0 + gate * (1.0 - sigma))).astype(BF16)
    up_grad[...] = (hidden_grad * gate * sigma).astype(BF16)

    for k in range(3):
        total_l.store(k * rank, exact_dot(total_p.load(k * rank, rank), lefts[k][...], NN) * (1.0 / tokens))
    total_l.scatter()
    total_l.gather()
    total_l.wait()

    for k in range(3):
        raw = total_l.load(k * rank, rank)
        total_m.store(k * rank, exact_dot(raw, lefts[k][...], NT))
        gram_own[k] = lax.dot_general(raw, raw, NT, precision=HIGH, preferred_element_type=F32)
    total_m.scatter()
    for step in range(1, n_tp):
        copy = pltpu.make_async_remote_copy(
            src_ref=gram_own, dst_ref=gram_come.at[step - 1],
            send_sem=gram_sems.at[0, step - 1], recv_sem=gram_sems.at[1, step - 1],
            device_id={"tensor": lax.rem(z + step, n_tp)}, device_id_type=MESH,
        )
        copy.start()
        gram_copies.append(copy)
    total_m.gather()
    total_m.wait()

    for k in range(3):
        total_r.store(k * rank, exact_dot(total_m.load(k * rank, rank), right(k), NN))
    total_r.scatter()

    gram = gram_own[...]
    for step in range(1, n_tp):
        gram_copies[step - 1].wait_recv()
        gram = gram + gram_come[step - 1]
    inverse = inverse_cholesky(gram)
    for k in range(3):
        left_out[k] = lax.dot_general(
            inverse[k], total_l.load(k * rank, rank), NN, precision=HIGH, preferred_element_type=F32
        )

    total_r.gather()
    total_r.wait()
    for k in range(3):
        right_out[k] = lax.dot_general(
            inverse[k], total_r.load(k * rank, rank), NN, precision=HIGH, preferred_element_type=F32
        ) * (1.0 / (tokens * n_dp))

    finish()


def exchange_scratch(count, rows, width):
    share = rows // count
    return [
        pltpu.VMEM((count, share, width), F32),
        pltpu.VMEM((count - 1, share, width), F32),
        pltpu.VMEM((count, share, width), F32),
        pltpu.SemaphoreType.DMA((4, count - 1)),
    ]


def shards(n_dp, n_tp, inputs, grad_out, gate_pre, up_pre, down_weight, warm_start):
    tokens, own = inputs.shape
    hidden_units, weight_columns = down_weight.shape
    count, _, rank = warm_start.shape
    halves = 2 if weight_columns % 256 == 0 else 1
    vmem = pl.BlockSpec(memory_space=pltpu.VMEM)
    loads = 4 + halves + n_dp // n_tp
    left, right = pl.pallas_call(
        functools.partial(kernel, n_dp, n_tp),
        out_shape=(
            jax.ShapeDtypeStruct((count, rank, hidden_units), F32),
            jax.ShapeDtypeStruct((count, rank, own), F32),
        ),
        in_specs=[pl.BlockSpec(memory_space=pl.ANY)] * 6,
        out_specs=(vmem, vmem),
        scratch_shapes=[
            pltpu.VMEM(inputs.shape, BF16),
            pltpu.VMEM(gate_pre.shape, BF16),
            pltpu.VMEM(up_pre.shape, BF16),
            pltpu.VMEM((count, rank, own), F32),
            pltpu.SemaphoreType.DMA((loads,)),
            pltpu.VMEM((n_dp, halves, hidden_units, weight_columns // halves), BF16),
            pltpu.SemaphoreType.DMA((n_dp, halves)),
            pltpu.SemaphoreType.DMA((n_dp, halves)),
            pltpu.VMEM((n_dp, tokens, weight_columns), BF16),
            pltpu.SemaphoreType.DMA((2, n_tp - 1)),
            pltpu.SemaphoreType.DMA((2, n_tp - 1)),
            pltpu.VMEM((tokens, hidden_units), F32),
            pltpu.VMEM((tokens, hidden_units), BF16),
            pltpu.VMEM((tokens, hidden_units), BF16),
            pltpu.VMEM((tokens, hidden_units), BF16),
            *exchange_scratch(n_tp, count * rank, tokens),
            *exchange_scratch(n_dp, count * rank, hidden_units),
            *exchange_scratch(n_tp, count * rank, tokens),
            *exchange_scratch(n_dp, count * rank, own),
            pltpu.VMEM((count, rank, rank), F32),
            pltpu.VMEM((n_tp - 1, count, rank, rank), F32),
            pltpu.SemaphoreType.DMA((2, n_tp - 1)),
        ],
        compiler_params=pltpu.CompilerParams(
            collective_id=0, has_side_effects=True, vmem_limit_bytes=56 * 1024 * 1024
        ),
        name="powersgd",
    )(inputs, grad_out, gate_pre, up_pre, down_weight, jnp.swapaxes(warm_start, 1, 2))
    return jnp.swapaxes(left, 1, 2), jnp.swapaxes(right, 1, 2)


def solution(mesh):
    placed = (
        P("dp", "tensor"),
        P("dp", "tensor"),
        P("dp", "tensor"),
        P("dp", "tensor"),
        P("tensor", "dp"),
        P(None, "tensor", None),
    )
    return jax.shard_map(
        functools.partial(shards, mesh.shape["dp"], mesh.shape["tensor"]),
        mesh=mesh,
        in_specs=placed,
        out_specs=(P(None, "tensor", None), P(None, "tensor", None)),
        check_vma=False,
    )
```

```python
import functools

import jax
import jax.numpy as jnp
from jax import lax
from jax.experimental import pallas as pl
from jax.experimental.pallas import tpu as pltpu
from jax.sharding import PartitionSpec as P

F32 = jnp.float32
BF16 = jnp.bfloat16
MESH = pl.DeviceIdType.MESH
HIGH = lax.Precision.HIGHEST
NN = (((1,), (0,)), ((), ()))
NT = (((1,), (1,)), ((), ()))


def flipped(index, mask):
    result, bit = index, 0
    while (1 << bit) <= mask:
        if mask & (1 << bit):
            result = result + (1 << bit) * (1 - 2 * (lax.div(index, 1 << bit) % 2))
        bit += 1
    return result


def exact_dot(left, right, dims):
    rows = left.shape[0]
    first = left.astype(BF16)
    rest = left - first.astype(F32)
    second = rest.astype(BF16)
    third = (rest - second.astype(F32)).astype(BF16)
    out = lax.dot_general(
        jnp.concatenate([first, second, third], axis=0), right, dims, preferred_element_type=F32
    )
    return out[:rows] + (out[rows : 2 * rows] + out[2 * rows :])


def inverse_cholesky(gram):
    count, rank, _ = gram.shape
    row_id = lax.broadcasted_iota(jnp.int32, (count, rank, rank), 1)
    col_id = lax.broadcasted_iota(jnp.int32, (count, rank, rank), 2)
    work = jnp.concatenate([(row_id == col_id).astype(F32), gram], axis=2)
    row_wide = lax.broadcasted_iota(jnp.int32, work.shape, 1)
    scale = jnp.zeros((count, rank, 1), F32)
    row_thin = lax.broadcasted_iota(jnp.int32, scale.shape, 1)
    for step in range(rank):
        row = work[:, step : step + 1, :]
        pivot = work[:, step : step + 1, rank + step : rank + step + 1]
        scale = jnp.where(row_thin == step, lax.rsqrt(pivot), scale)
        if step < rank - 1:
            column = work[:, :, rank + step : rank + step + 1]
            factor = column / pivot
            work = work - jnp.where(row_wide > step, factor * row, 0.0)
    return work[:, :, :rank] * scale


class Exchange:
    def __init__(self, axis, count, refs):
        self.axis, self.count = axis, count
        self.part, self.come, self.full, self.sems = refs
        self.me = lax.axis_index(axis)
        self.copies, self.later = [], []

    def store(self, row, value):
        share = self.part.shape[1]
        done = 0
        while done < value.shape[0]:
            index, offset = (row + done) // share, (row + done) % share
            size = min(share - offset, value.shape[0] - done)
            self.part[index, offset : offset + size, :] = value[done : done + size]
            done += size

    def scatter(self):
        for step in range(1, self.count):
            peer = lax.rem(self.me + step, self.count)
            copy = pltpu.make_async_remote_copy(
                src_ref=self.part.at[peer],
                dst_ref=self.come.at[step - 1],
                send_sem=self.sems.at[0, step - 1],
                recv_sem=self.sems.at[1, step - 1],
                device_id={self.axis: peer},
                device_id_type=MESH,
            )
            copy.start()
            self.copies.append(copy)

    def gather(self):
        total = self.part[self.me]
        for step in range(1, self.count):
            self.copies[step - 1].wait_recv()
            total = total + self.come[step - 1]
        self.full[self.me] = total
        for step in range(1, self.count):
            peer = lax.rem(self.me + step, self.count)
            copy = pltpu.make_async_remote_copy(
                src_ref=self.full.at[self.me],
                dst_ref=self.full.at[self.me],
                send_sem=self.sems.at[2, step - 1],
                recv_sem=self.sems.at[3, step - 1],
                device_id={self.axis: peer},
                device_id_type=MESH,
            )
            copy.start()
            self.later.append(copy)

    def wait(self):
        for step in range(1, self.count):
            source = lax.rem(self.me + self.count - step, self.count)
            pltpu.make_async_remote_copy(
                src_ref=self.full.at[source],
                dst_ref=self.full.at[source],
                send_sem=self.sems.at[2, step - 1],
                recv_sem=self.sems.at[3, step - 1],
                device_id={self.axis: lax.rem(self.me + step, self.count)},
                device_id_type=MESH,
            ).wait_recv()

    def load(self, row, size):
        share = self.full.shape[1]
        pieces, done = [], 0
        while done < size:
            index, offset = (row + done) // share, (row + done) % share
            take = min(share - offset, size - done)
            pieces.append(self.full[index, offset : offset + take, :])
            done += take
        return jnp.concatenate(pieces, axis=0)

    def finish(self):
        for copy in self.copies + self.later:
            copy.wait_send()


def kernel(n_dp, n_tp, x_hbm, g_hbm, gate_hbm, up_hbm, w_hbm, warm_hbm, left_out, right_out,
           x_ref, gate_ref, up_ref, warm_ref, load_sems, wbuf, wsend, wrecv, gfull, gsend, grecv, hg, gate_slope, up_slope, gate_grad, up_grad, hidden,
           p0, p1, p2, p3, l0, l1, l2, l3, m0, m1, m2, m3, r0, r1, r2, r3,
           gram_own, gram_come, gram_sems):
    d, z = lax.axis_index("dp"), lax.axis_index("tensor")
    tokens = x_ref.shape[0]
    rank = warm_ref.shape[1]
    weight_columns = w_hbm.shape[1]
    per = n_dp // n_tp
    halves = wsend.shape[1]
    width = weight_columns // halves
    bits = n_dp.bit_length() - 1

    barrier = pltpu.get_barrier_semaphore()
    for step in range(1, n_dp):
        pl.semaphore_signal(barrier, inc=1, device_id={"dp": lax.rem(d + step, n_dp)}, device_id_type=MESH)
    for step in range(1, n_tp):
        pl.semaphore_signal(barrier, inc=1, device_id={"tensor": lax.rem(z + step, n_tp)}, device_id_type=MESH)

    loads = []

    def load(source, target):
        copy = pltpu.make_async_copy(source, target, load_sems.at[len(loads)])
        copy.start()
        loads.append(copy)
        return copy

    load_g = [
        load(g_hbm.at[:, pl.ds(part * weight_columns, weight_columns)], gfull.at[z * per + part])
        for part in range(per)
    ]
    load_w = [
        load(w_hbm.at[:, pl.ds(half * width, width)], wbuf.at[d, :, pl.ds(half * width, width)])
        for half in range(halves)
    ]
    load_warm, load_x = load(warm_hbm, warm_ref), load(x_hbm, x_ref)
    load_gate, load_up = load(gate_hbm, gate_ref), load(up_hbm, up_ref)
    for copy in load_g:
        copy.wait()
    pl.semaphore_wait(barrier, n_dp - 1 + n_tp - 1)

    def shard(index):
        return gfull.at[pl.ds(index * per, per)]

    def line_copy(way, hop):
        source = z - hop if way == 0 else z + hop
        target = z + 1 if way == 0 else z - 1
        return pltpu.make_async_remote_copy(
            src_ref=shard(source), dst_ref=shard(source),
            send_sem=gsend.at[way, hop], recv_sem=grecv.at[way, hop],
            device_id={"tensor": target}, device_id_type=MESH,
        )

    def line_sends(way, hop):
        if way == 0:
            return jnp.logical_and(z - hop >= 0, z < n_tp - 1)
        return jnp.logical_and(z + hop <= n_tp - 1, z > 0)

    def line_start(hop):
        for way in (0, 1):
            @pl.when(line_sends(way, hop))
            def _():
                line_copy(way, hop).start()

    def line_wait(hop):
        for way in (0, 1):
            source = z - 1 - hop if way == 0 else z + 1 + hop
            @pl.when(source >= 0 if way == 0 else source <= n_tp - 1)
            def _():
                pltpu.make_async_remote_copy(
                    src_ref=shard(source), dst_ref=shard(source),
                    send_sem=gsend.at[way, hop], recv_sem=grecv.at[way, hop],
                    device_id={"tensor": z - 1 if way == 0 else z + 1}, device_id_type=MESH,
                ).wait_recv()

    orders = [list(range(1, bits)) + [0], list(range(bits - 1, 0, -1)) + [0]]
    weight_copies = []

    def weight_copy(slot, half, partner, sem_slot):
        place = wbuf.at[flipped(d, slot), :, pl.ds(half * width, width)]
        return pltpu.make_async_remote_copy(
            src_ref=place, dst_ref=place,
            send_sem=wsend.at[sem_slot, half], recv_sem=wrecv.at[sem_slot, half],
            device_id={"dp": flipped(d, partner)}, device_id_type=MESH,
        )

    def weight_send(slot, half, first):
        for bit in orders[half][first:]:
            copy = weight_copy(slot, half, 1 << bit, slot ^ (1 << bit))
            copy.start()
            weight_copies.append(copy)

    def weight_wave(position):
        for index in range(1 << position):
            for half in range(halves):
                order = orders[half]
                slot = 1 << order[position]
                for place in range(position):
                    if index & (1 << place):
                        slot |= 1 << order[place]
                weight_copy(slot, half, 1 << order[position], slot).wait_recv()
                weight_send(slot, half, position + 1)

    gram_copies = []

    def finish():
        for exchange in (total_p, total_l, total_m, total_r):
            exchange.finish()
        for copy in gram_copies + weight_copies:
            copy.wait_send()
        for hop in range(n_tp - 1):
            for way in (0, 1):
                @pl.when(line_sends(way, hop))
                def _():
                    line_copy(way, hop).wait_send()

    line_start(0)
    for half in range(halves):
        load_w[half].wait()
        weight_send(0, half, 0)

    total_p = Exchange("tensor", n_tp, (p0, p1, p2, p3))
    total_l = Exchange("dp", n_dp, (l0, l1, l2, l3))
    total_m = Exchange("tensor", n_tp, (m0, m1, m2, m3))
    total_r = Exchange("dp", n_dp, (r0, r1, r2, r3))
    lefts = (gate_grad, up_grad, hidden)

    def right(k):
        if k < 2:
            return x_ref[...]
        return jnp.concatenate([gfull[z * per + part] for part in range(per)], axis=1)

    load_warm.wait()
    load_x.wait()
    for k in range(3):
        total_p.store(k * rank, exact_dot(warm_ref[k], right(k), NT))
    total_p.scatter()

    load_gate.wait()
    load_up.wait()
    gate = gate_ref[...].astype(F32)
    up = up_ref[...].astype(F32)
    sigma = 1.0 / (1.0 + jnp.exp(-gate))
    hidden[...] = (gate * sigma * up).astype(BF16)
    gate_slope[...] = up * sigma * (1.0 + gate * (1.0 - sigma))
    up_slope[...] = gate * sigma

    def product(source):
        total = None
        for part in range(per):
            block = source * per + part
            term = lax.dot_general(gfull[block], wbuf[block], NT, preferred_element_type=F32)
            total = term if total is None else total + term
        return total

    def line_use(hop):
        for way in (0, 1):
            source = z - 1 - hop if way == 0 else z + 1 + hop
            @pl.when(source >= 0 if way == 0 else source <= n_tp - 1)
            def _():
                hg[...] += product(source)

    last = n_tp - 2
    waves = list(range(bits - 1))
    for hop in range(last):
        line_wait(hop)
        line_start(hop + 1)
        if waves:
            weight_wave(waves.pop(0))
        if hop == 0:
            total_p.gather()
    for position in waves:
        weight_wave(position)
    total_p.wait()
    weight_wave(bits - 1)
    hg[...] = product(z)
    for hop in range(last):
        line_use(hop)
    line_wait(last)
    line_use(last)

    hidden_grad = hg[...]
    gate_grad[...] = (hidden_grad * gate_slope[...]).astype(BF16)
    up_grad[...] = (hidden_grad * up_slope[...]).astype(BF16)

    for k in range(3):
        total_l.store(k * rank, exact_dot(total_p.load(k * rank, rank), lefts[k][...], NN) * (1.0 / tokens))
    total_l.scatter()
    total_l.gather()
    total_l.wait()

    gram_own[...] = jnp.zeros_like(gram_own)
    for k in range(3):
        raw = total_l.load(k * rank, rank)
        total_m.store(k * rank, exact_dot(raw, lefts[k][...], NT))
        gram_own[:, k * rank : (k + 1) * rank] = lax.dot_general(raw, raw, NT, precision=HIGH, preferred_element_type=F32)
    total_m.scatter()
    for step in range(1, n_tp):
        copy = pltpu.make_async_remote_copy(
            src_ref=gram_own, dst_ref=gram_come.at[step - 1],
            send_sem=gram_sems.at[0, step - 1], recv_sem=gram_sems.at[1, step - 1],
            device_id={"tensor": lax.rem(z + step, n_tp)}, device_id_type=MESH,
        )
        copy.start()
        gram_copies.append(copy)
    total_m.gather()
    total_m.wait()

    for k in range(3):
        total_r.store(k * rank, exact_dot(total_m.load(k * rank, rank), right(k), NN))
    total_r.scatter()

    gram = gram_own[:, : 3 * rank]
    for step in range(1, n_tp):
        gram_copies[step - 1].wait_recv()
        gram = gram + gram_come[step - 1, :, : 3 * rank]
    inverse = inverse_cholesky(
        jnp.stack([gram[:, k * rank : (k + 1) * rank] for k in range(3)])
    )
    total_r.gather()
    for k in range(3):
        left_out[k] = lax.dot_general(
            inverse[k], total_l.load(k * rank, rank), NN, precision=HIGH, preferred_element_type=F32
        )

    total_r.wait()
    for k in range(3):
        right_out[k] = lax.dot_general(
            inverse[k], total_r.load(k * rank, rank), NN, precision=HIGH, preferred_element_type=F32
        ) * (1.0 / (tokens * n_dp))

    finish()


def exchange_scratch(count, rows, width):
    share = rows // count
    return [
        pltpu.VMEM((count, share, width), F32),
        pltpu.VMEM((count - 1, share, width), F32),
        pltpu.VMEM((count, share, width), F32),
        pltpu.SemaphoreType.DMA((4, count - 1)),
    ]


def shards(n_dp, n_tp, inputs, grad_out, gate_pre, up_pre, down_weight, warm_start):
    tokens, own = inputs.shape
    hidden_units, weight_columns = down_weight.shape
    count, _, rank = warm_start.shape
    halves = 2 if weight_columns % 256 == 0 else 1
    vmem = pl.BlockSpec(memory_space=pltpu.VMEM)
    gram_width = pl.cdiv(count * rank, 128) * 128
    loads = 4 + halves + n_dp // n_tp
    left, right = pl.pallas_call(
        functools.partial(kernel, n_dp, n_tp),
        out_shape=(
            jax.ShapeDtypeStruct((count, rank, hidden_units), F32),
            jax.ShapeDtypeStruct((count, rank, own), F32),
        ),
        in_specs=[pl.BlockSpec(memory_space=pl.ANY)] * 6,
        out_specs=(vmem, vmem),
        scratch_shapes=[
            pltpu.VMEM(inputs.shape, BF16),
            pltpu.VMEM(gate_pre.shape, BF16),
            pltpu.VMEM(up_pre.shape, BF16),
            pltpu.VMEM((count, rank, own), F32),
            pltpu.SemaphoreType.DMA((loads,)),
            pltpu.VMEM((n_dp, hidden_units, weight_columns), BF16),
            pltpu.SemaphoreType.DMA((n_dp, halves)),
            pltpu.SemaphoreType.DMA((n_dp, halves)),
            pltpu.VMEM((n_dp, tokens, weight_columns), BF16),
            pltpu.SemaphoreType.DMA((2, n_tp - 1)),
            pltpu.SemaphoreType.DMA((2, n_tp - 1)),
            pltpu.VMEM((tokens, hidden_units), F32),
            pltpu.VMEM((tokens, hidden_units), F32),
            pltpu.VMEM((tokens, hidden_units), F32),
            pltpu.VMEM((tokens, hidden_units), BF16),
            pltpu.VMEM((tokens, hidden_units), BF16),
            pltpu.VMEM((tokens, hidden_units), BF16),
            *exchange_scratch(n_tp, count * rank, tokens),
            *exchange_scratch(n_dp, count * rank, hidden_units),
            *exchange_scratch(n_tp, count * rank, tokens),
            *exchange_scratch(n_dp, count * rank, own),
            pltpu.VMEM((rank, gram_width), F32),
            pltpu.VMEM((n_tp - 1, rank, gram_width), F32),
            pltpu.SemaphoreType.DMA((2, n_tp - 1)),
        ],
        compiler_params=pltpu.CompilerParams(
            collective_id=0, has_side_effects=True, vmem_limit_bytes=56 * 1024 * 1024
        ),
        name="powersgd",
    )(inputs, grad_out, gate_pre, up_pre, down_weight, jnp.swapaxes(warm_start, 1, 2))
    return jnp.swapaxes(left, 1, 2), jnp.swapaxes(right, 1, 2)


def solution(mesh):
    placed = (
        P("dp", "tensor"),
        P("dp", "tensor"),
        P("dp", "tensor"),
        P("dp", "tensor"),
        P("tensor", "dp"),
        P(None, "tensor", None),
    )
    return jax.shard_map(
        functools.partial(shards, mesh.shape["dp"], mesh.shape["tensor"]),
        mesh=mesh,
        in_specs=placed,
        out_specs=(P(None, "tensor", None), P(None, "tensor", None)),
        check_vma=False,
    )
```

```python
import functools

import jax
import jax.numpy as jnp
from jax import lax
from jax.experimental import pallas as pl
from jax.experimental.pallas import tpu as pltpu
from jax.sharding import PartitionSpec as P

F32 = jnp.float32
BF16 = jnp.bfloat16
MESH = pl.DeviceIdType.MESH
HIGH = lax.Precision.HIGHEST
NN = (((1,), (0,)), ((), ()))
NT = (((1,), (1,)), ((), ()))


def flipped(index, mask):
    result, bit = index, 0
    while (1 << bit) <= mask:
        if mask & (1 << bit):
            result = result + (1 << bit) * (1 - 2 * (lax.div(index, 1 << bit) % 2))
        bit += 1
    return result


def exact_dot(left, right, dims):
    rows = left.shape[0]
    first = left.astype(BF16)
    rest = left - first.astype(F32)
    second = rest.astype(BF16)
    third = (rest - second.astype(F32)).astype(BF16)
    out = lax.dot_general(
        jnp.concatenate([first, second, third], axis=0), right, dims, preferred_element_type=F32
    )
    return out[:rows] + (out[rows : 2 * rows] + out[2 * rows :])


def inverse_cholesky(gram):
    count, rank, _ = gram.shape
    row_id = lax.broadcasted_iota(jnp.int32, (count, rank, rank), 1)
    col_id = lax.broadcasted_iota(jnp.int32, (count, rank, rank), 2)
    work = jnp.concatenate([(row_id == col_id).astype(F32), gram], axis=2)
    row_wide = lax.broadcasted_iota(jnp.int32, work.shape, 1)
    scale = jnp.zeros((count, rank, 1), F32)
    row_thin = lax.broadcasted_iota(jnp.int32, scale.shape, 1)
    for step in range(rank):
        row = work[:, step : step + 1, :]
        pivot = work[:, step : step + 1, rank + step : rank + step + 1]
        scale = jnp.where(row_thin == step, lax.rsqrt(pivot), scale)
        if step < rank - 1:
            column = work[:, :, rank + step : rank + step + 1]
            factor = column / pivot
            work = work - jnp.where(row_wide > step, factor * row, 0.0)
    return work[:, :, :rank] * scale


class Exchange:
    def __init__(self, axis, count, refs):
        self.axis, self.count = axis, count
        self.part, self.come, self.full, self.sems = refs
        self.me = lax.axis_index(axis)
        self.copies, self.later = [], []

    def store(self, row, value):
        share = self.part.shape[1]
        done = 0
        while done < value.shape[0]:
            index, offset = (row + done) // share, (row + done) % share
            size = min(share - offset, value.shape[0] - done)
            self.part[index, offset : offset + size, :] = value[done : done + size]
            done += size

    def scatter(self):
        for step in range(1, self.count):
            peer = lax.rem(self.me + step, self.count)
            copy = pltpu.make_async_remote_copy(
                src_ref=self.part.at[peer],
                dst_ref=self.come.at[step - 1],
                send_sem=self.sems.at[0, step - 1],
                recv_sem=self.sems.at[1, step - 1],
                device_id={self.axis: peer},
                device_id_type=MESH,
            )
            copy.start()
            self.copies.append(copy)

    def gather(self):
        total = self.part[self.me]
        for step in range(1, self.count):
            self.copies[step - 1].wait_recv()
            total = total + self.come[step - 1]
        self.full[self.me] = total
        for step in range(1, self.count):
            peer = lax.rem(self.me + step, self.count)
            copy = pltpu.make_async_remote_copy(
                src_ref=self.full.at[self.me],
                dst_ref=self.full.at[self.me],
                send_sem=self.sems.at[2, step - 1],
                recv_sem=self.sems.at[3, step - 1],
                device_id={self.axis: peer},
                device_id_type=MESH,
            )
            copy.start()
            self.later.append(copy)

    def wait(self):
        for step in range(1, self.count):
            source = lax.rem(self.me + self.count - step, self.count)
            pltpu.make_async_remote_copy(
                src_ref=self.full.at[source],
                dst_ref=self.full.at[source],
                send_sem=self.sems.at[2, step - 1],
                recv_sem=self.sems.at[3, step - 1],
                device_id={self.axis: lax.rem(self.me + step, self.count)},
                device_id_type=MESH,
            ).wait_recv()

    def load(self, row, size):
        share = self.full.shape[1]
        pieces, done = [], 0
        while done < size:
            index, offset = (row + done) // share, (row + done) % share
            take = min(share - offset, size - done)
            pieces.append(self.full[index, offset : offset + take, :])
            done += take
        return jnp.concatenate(pieces, axis=0)

    def finish(self):
        for copy in self.copies + self.later:
            copy.wait_send()


def kernel(n_dp, n_tp, x_hbm, g_hbm, gate_hbm, up_hbm, w_hbm, warm_hbm, left_out, right_out,
           x_ref, gate_ref, up_ref, warm_ref, load_sems, wbuf, wsend, wrecv, gfull, gsend, grecv, hg, gate_slope, up_slope, gate_grad, up_grad, hidden,
           gram_own, gram_come, gram_sems, *exchange_refs):
    d, z = lax.axis_index("dp"), lax.axis_index("tensor")
    tokens = x_ref.shape[0]
    rank = warm_ref.shape[1]
    weight_columns = w_hbm.shape[1]
    per = n_dp // n_tp
    halves = wsend.shape[1]
    width = weight_columns // halves
    bits = n_dp.bit_length() - 1

    barrier = pltpu.get_barrier_semaphore()
    for step in range(1, n_dp):
        pl.semaphore_signal(barrier, inc=1, device_id={"dp": lax.rem(d + step, n_dp)}, device_id_type=MESH)
    for step in range(1, n_tp):
        pl.semaphore_signal(barrier, inc=1, device_id={"tensor": lax.rem(z + step, n_tp)}, device_id_type=MESH)

    loads = []

    def load(source, target):
        copy = pltpu.make_async_copy(source, target, load_sems.at[len(loads)])
        copy.start()
        loads.append(copy)
        return copy

    load_g = [
        load(g_hbm.at[:, pl.ds(part * weight_columns, weight_columns)], gfull.at[z * per + part])
        for part in range(per)
    ]
    load_w = [
        load(w_hbm.at[:, pl.ds(half * width, width)], wbuf.at[d, :, pl.ds(half * width, width)])
        for half in range(halves)
    ]
    load_warm, load_x = load(warm_hbm, warm_ref), load(x_hbm, x_ref)
    load_gate, load_up = load(gate_hbm, gate_ref), load(up_hbm, up_ref)
    for copy in load_g:
        copy.wait()
    pl.semaphore_wait(barrier, n_dp - 1 + n_tp - 1)

    def shard(index):
        return gfull.at[pl.ds(index * per, per)]

    def line_copy(way, hop):
        source = z - hop if way == 0 else z + hop
        target = z + 1 if way == 0 else z - 1
        return pltpu.make_async_remote_copy(
            src_ref=shard(source), dst_ref=shard(source),
            send_sem=gsend.at[way, hop], recv_sem=grecv.at[way, hop],
            device_id={"tensor": target}, device_id_type=MESH,
        )

    def line_sends(way, hop):
        if way == 0:
            return jnp.logical_and(z - hop >= 0, z < n_tp - 1)
        return jnp.logical_and(z + hop <= n_tp - 1, z > 0)

    def line_start(hop):
        for way in (0, 1):
            @pl.when(line_sends(way, hop))
            def _():
                line_copy(way, hop).start()

    def line_wait(hop):
        for way in (0, 1):
            source = z - 1 - hop if way == 0 else z + 1 + hop
            @pl.when(source >= 0 if way == 0 else source <= n_tp - 1)
            def _():
                pltpu.make_async_remote_copy(
                    src_ref=shard(source), dst_ref=shard(source),
                    send_sem=gsend.at[way, hop], recv_sem=grecv.at[way, hop],
                    device_id={"tensor": z - 1 if way == 0 else z + 1}, device_id_type=MESH,
                ).wait_recv()

    orders = [list(range(1, bits)) + [0], list(range(bits - 1, 0, -1)) + [0]]
    weight_copies = []

    def weight_copy(slot, half, partner, sem_slot):
        place = wbuf.at[flipped(d, slot), :, pl.ds(half * width, width)]
        return pltpu.make_async_remote_copy(
            src_ref=place, dst_ref=place,
            send_sem=wsend.at[sem_slot, half], recv_sem=wrecv.at[sem_slot, half],
            device_id={"dp": flipped(d, partner)}, device_id_type=MESH,
        )

    def weight_send(slot, half, first):
        for bit in orders[half][first:]:
            copy = weight_copy(slot, half, 1 << bit, slot ^ (1 << bit))
            copy.start()
            weight_copies.append(copy)

    def weight_wave(position):
        for index in range(1 << position):
            for half in range(halves):
                order = orders[half]
                slot = 1 << order[position]
                for place in range(position):
                    if index & (1 << place):
                        slot |= 1 << order[place]
                weight_copy(slot, half, 1 << order[position], slot).wait_recv()
                weight_send(slot, half, position + 1)

    gram_copies = []

    def finish():
        for exchange in exchanges:
            exchange.finish()
        for copy in gram_copies + weight_copies:
            copy.wait_send()
        for hop in range(n_tp - 1):
            for way in (0, 1):
                @pl.when(line_sends(way, hop))
                def _():
                    line_copy(way, hop).wait_send()

    line_start(0)
    for half in range(halves):
        load_w[half].wait()
        weight_send(0, half, 0)

    total_p, left_pair, left_last, mid_pair, mid_last, right_pair, right_last = exchanges = [
        Exchange(axis, count, exchange_refs[4 * index : 4 * index + 4])
        for index, (axis, count) in enumerate(
            [("tensor", n_tp)] + [("dp", n_dp)] * 2 + [("tensor", n_tp)] * 2 + [("dp", n_dp)] * 2
        )
    ]
    lefts = (gate_grad, up_grad, hidden)

    def right(k):
        if k < 2:
            return x_ref[...]
        return jnp.concatenate([gfull[z * per + part] for part in range(per)], axis=1)

    load_warm.wait()
    load_x.wait()
    for k in range(3):
        total_p.store(k * rank, exact_dot(warm_ref[k], right(k), NT))
    total_p.scatter()

    load_gate.wait()
    load_up.wait()
    gate = gate_ref[...].astype(F32)
    up = up_ref[...].astype(F32)
    sigma = 1.0 / (1.0 + jnp.exp(-gate))
    hidden[...] = (gate * sigma * up).astype(BF16)
    gate_slope[...] = up * sigma * (1.0 + gate * (1.0 - sigma))
    up_slope[...] = gate * sigma

    def product(source):
        total = None
        for part in range(per):
            block = source * per + part
            term = lax.dot_general(gfull[block], wbuf[block], NT, preferred_element_type=F32)
            total = term if total is None else total + term
        return total

    def line_use(hop):
        for way in (0, 1):
            source = z - 1 - hop if way == 0 else z + 1 + hop
            @pl.when(source >= 0 if way == 0 else source <= n_tp - 1)
            def _():
                hg[...] += product(source)

    last = n_tp - 2
    waves = list(range(bits - 1))
    for hop in range(last):
        line_wait(hop)
        line_start(hop + 1)
        if waves:
            weight_wave(waves.pop(0))
        if hop == 0:
            total_p.gather()
    for position in waves:
        weight_wave(position)
    total_p.wait()

    def left_part(k):
        return exact_dot(total_p.load(k * rank, rank), lefts[k][...], NN) * (1.0 / tokens)

    left_last.store(0, left_part(2))
    left_last.scatter()
    weight_wave(bits - 1)
    hg[...] = product(z)
    for hop in range(last):
        line_use(hop)
    left_last.gather()
    line_wait(last)
    line_use(last)

    hidden_grad = hg[...]
    gate_grad[...] = (hidden_grad * gate_slope[...]).astype(BF16)
    up_grad[...] = (hidden_grad * up_slope[...]).astype(BF16)

    for k in range(2):
        left_pair.store(k * rank, left_part(k))
    left_pair.scatter()

    left_last.wait()
    mid_last.store(0, exact_dot(left_last.load(0, rank), hidden[...], NT))
    mid_last.scatter()
    left_pair.gather()
    mid_last.gather()
    left_pair.wait()
    raws = [left_pair.load(0, rank), left_pair.load(rank, rank), left_last.load(0, rank)]
    for k in range(2):
        mid_pair.store(k * rank, exact_dot(raws[k], lefts[k][...], NT))
    mid_pair.scatter()
    gram_own[...] = jnp.zeros_like(gram_own)
    for k in range(3):
        gram_own[:, k * rank : (k + 1) * rank] = lax.dot_general(
            raws[k], raws[k], NT, precision=HIGH, preferred_element_type=F32
        )
    for step in range(1, n_tp):
        copy = pltpu.make_async_remote_copy(
            src_ref=gram_own, dst_ref=gram_come.at[step - 1],
            send_sem=gram_sems.at[0, step - 1], recv_sem=gram_sems.at[1, step - 1],
            device_id={"tensor": lax.rem(z + step, n_tp)}, device_id_type=MESH,
        )
        copy.start()
        gram_copies.append(copy)

    mid_last.wait()
    right_last.store(0, exact_dot(mid_last.load(0, rank), right(2), NN))
    right_last.scatter()
    mid_pair.gather()
    right_last.gather()
    mid_pair.wait()
    for k in range(2):
        right_pair.store(k * rank, exact_dot(mid_pair.load(k * rank, rank), right(k), NN))
    right_pair.scatter()

    gram = gram_own[:, : 3 * rank]
    for step in range(1, n_tp):
        gram_copies[step - 1].wait_recv()
        gram = gram + gram_come[step - 1, :, : 3 * rank]
    inverse = inverse_cholesky(
        jnp.stack([gram[:, k * rank : (k + 1) * rank] for k in range(3)])
    )
    right_pair.gather()

    def orthogonal(k, raw):
        return lax.dot_general(inverse[k], raw, NN, precision=HIGH, preferred_element_type=F32)

    for k in range(3):
        left_out[k] = orthogonal(k, raws[k])
    right_last.wait()
    right_out[2] = orthogonal(2, right_last.load(0, rank)) * (1.0 / (tokens * n_dp))
    right_pair.wait()
    for k in range(2):
        right_out[k] = orthogonal(k, right_pair.load(k * rank, rank)) * (1.0 / (tokens * n_dp))

    finish()


def exchange_scratch(count, rows, width):
    share = rows // count
    return [
        pltpu.VMEM((count, share, width), F32),
        pltpu.VMEM((count - 1, share, width), F32),
        pltpu.VMEM((count, share, width), F32),
        pltpu.SemaphoreType.DMA((4, count - 1)),
    ]


def shards(n_dp, n_tp, inputs, grad_out, gate_pre, up_pre, down_weight, warm_start):
    tokens, own = inputs.shape
    hidden_units, weight_columns = down_weight.shape
    count, _, rank = warm_start.shape
    halves = 2 if weight_columns % 256 == 0 else 1
    vmem = pl.BlockSpec(memory_space=pltpu.VMEM)
    gram_width = pl.cdiv(count * rank, 128) * 128
    loads = 4 + halves + n_dp // n_tp
    left, right = pl.pallas_call(
        functools.partial(kernel, n_dp, n_tp),
        out_shape=(
            jax.ShapeDtypeStruct((count, rank, hidden_units), F32),
            jax.ShapeDtypeStruct((count, rank, own), F32),
        ),
        in_specs=[pl.BlockSpec(memory_space=pl.ANY)] * 6,
        out_specs=(vmem, vmem),
        scratch_shapes=[
            pltpu.VMEM(inputs.shape, BF16),
            pltpu.VMEM(gate_pre.shape, BF16),
            pltpu.VMEM(up_pre.shape, BF16),
            pltpu.VMEM((count, rank, own), F32),
            pltpu.SemaphoreType.DMA((loads,)),
            pltpu.VMEM((n_dp, hidden_units, weight_columns), BF16),
            pltpu.SemaphoreType.DMA((n_dp, halves)),
            pltpu.SemaphoreType.DMA((n_dp, halves)),
            pltpu.VMEM((n_dp, tokens, weight_columns), BF16),
            pltpu.SemaphoreType.DMA((2, n_tp - 1)),
            pltpu.SemaphoreType.DMA((2, n_tp - 1)),
            pltpu.VMEM((tokens, hidden_units), F32),
            pltpu.VMEM((tokens, hidden_units), F32),
            pltpu.VMEM((tokens, hidden_units), F32),
            pltpu.VMEM((tokens, hidden_units), BF16),
            pltpu.VMEM((tokens, hidden_units), BF16),
            pltpu.VMEM((tokens, hidden_units), BF16),
            pltpu.VMEM((rank, gram_width), F32),
            pltpu.VMEM((n_tp - 1, rank, gram_width), F32),
            pltpu.SemaphoreType.DMA((2, n_tp - 1)),
            *exchange_scratch(n_tp, 3 * rank, tokens),
            *exchange_scratch(n_dp, 2 * rank, hidden_units),
            *exchange_scratch(n_dp, rank, hidden_units),
            *exchange_scratch(n_tp, 2 * rank, tokens),
            *exchange_scratch(n_tp, rank, tokens),
            *exchange_scratch(n_dp, 2 * rank, own),
            *exchange_scratch(n_dp, rank, own),
        ],
        compiler_params=pltpu.CompilerParams(
            collective_id=0, has_side_effects=True, vmem_limit_bytes=56 * 1024 * 1024
        ),
        name="powersgd",
    )(inputs, grad_out, gate_pre, up_pre, down_weight, jnp.swapaxes(warm_start, 1, 2))
    return jnp.swapaxes(left, 1, 2), jnp.swapaxes(right, 1, 2)


def solution(mesh):
    placed = (
        P("dp", "tensor"),
        P("dp", "tensor"),
        P("dp", "tensor"),
        P("dp", "tensor"),
        P("tensor", "dp"),
        P(None, "tensor", None),
    )
    return jax.shard_map(
        functools.partial(shards, mesh.shape["dp"], mesh.shape["tensor"]),
        mesh=mesh,
        in_specs=placed,
        out_specs=(P(None, "tensor", None), P(None, "tensor", None)),
        check_vma=False,
    )
```

```python
import functools

import jax
import jax.numpy as jnp
from jax import lax
from jax.experimental import pallas as pl
from jax.experimental.pallas import tpu as pltpu
from jax.sharding import PartitionSpec as P

F32 = jnp.float32
BF16 = jnp.bfloat16
MESH = pl.DeviceIdType.MESH
HIGH = lax.Precision.HIGHEST
NN = (((1,), (0,)), ((), ()))
NT = (((1,), (1,)), ((), ()))


def flipped(index, mask):
    result, bit = index, 0
    while (1 << bit) <= mask:
        if mask & (1 << bit):
            result = result + (1 << bit) * (1 - 2 * (lax.div(index, 1 << bit) % 2))
        bit += 1
    return result


def exact_dot(left, right, dims):
    rows = left.shape[0]
    first = left.astype(BF16)
    rest = left - first.astype(F32)
    second = rest.astype(BF16)
    third = (rest - second.astype(F32)).astype(BF16)
    out = lax.dot_general(
        jnp.concatenate([first, second, third], axis=0), right, dims, preferred_element_type=F32
    )
    return out[:rows] + (out[rows : 2 * rows] + out[2 * rows :])


class InverseCholesky:
    def __init__(self, gram):
        count, self.rank, _ = gram.shape
        row_id = lax.broadcasted_iota(jnp.int32, gram.shape, 1)
        col_id = lax.broadcasted_iota(jnp.int32, gram.shape, 2)
        self.work = jnp.concatenate([(row_id == col_id).astype(F32), gram], axis=2)
        self.row_wide = lax.broadcasted_iota(jnp.int32, self.work.shape, 1)
        self.scale = jnp.zeros((count, self.rank, 1), F32)
        self.row_thin = lax.broadcasted_iota(jnp.int32, self.scale.shape, 1)

    def run(self, first, end):
        for step in range(first, end):
            at = self.rank + step
            row = self.work[:, step : step + 1, :]
            pivot = self.work[:, step : step + 1, at : at + 1]
            self.scale = jnp.where(self.row_thin == step, lax.rsqrt(pivot), self.scale)
            if step < self.rank - 1:
                factor = self.work[:, :, at : at + 1] / pivot
                self.work = self.work - jnp.where(self.row_wide > step, factor * row, 0.0)

    def result(self):
        return self.work[:, :, : self.rank] * self.scale


class Exchange:
    def __init__(self, axis, count, refs):
        self.axis, self.count = axis, count
        self.part, self.come, self.full, self.sems = refs
        self.me = lax.axis_index(axis)
        self.copies, self.later = [], []

    def store(self, row, value):
        share = self.part.shape[1]
        done = 0
        while done < value.shape[0]:
            index, offset = (row + done) // share, (row + done) % share
            size = min(share - offset, value.shape[0] - done)
            self.part[index, offset : offset + size, :] = value[done : done + size]
            done += size

    def scatter(self):
        for step in range(1, self.count):
            peer = lax.rem(self.me + step, self.count)
            copy = pltpu.make_async_remote_copy(
                src_ref=self.part.at[peer],
                dst_ref=self.come.at[step - 1],
                send_sem=self.sems.at[0, step - 1],
                recv_sem=self.sems.at[1, step - 1],
                device_id={self.axis: peer},
                device_id_type=MESH,
            )
            copy.start()
            self.copies.append(copy)

    def gather(self):
        total = self.part[self.me]
        for step in range(1, self.count):
            self.copies[step - 1].wait_recv()
            total = total + self.come[step - 1]
        self.full[self.me] = total
        for step in range(1, self.count):
            peer = lax.rem(self.me + step, self.count)
            copy = pltpu.make_async_remote_copy(
                src_ref=self.full.at[self.me],
                dst_ref=self.full.at[self.me],
                send_sem=self.sems.at[2, step - 1],
                recv_sem=self.sems.at[3, step - 1],
                device_id={self.axis: peer},
                device_id_type=MESH,
            )
            copy.start()
            self.later.append(copy)

    def wait(self):
        for step in range(1, self.count):
            source = lax.rem(self.me + self.count - step, self.count)
            pltpu.make_async_remote_copy(
                src_ref=self.full.at[source],
                dst_ref=self.full.at[source],
                send_sem=self.sems.at[2, step - 1],
                recv_sem=self.sems.at[3, step - 1],
                device_id={self.axis: lax.rem(self.me + step, self.count)},
                device_id_type=MESH,
            ).wait_recv()

    def load(self, row, size):
        share = self.full.shape[1]
        pieces, done = [], 0
        while done < size:
            index, offset = (row + done) // share, (row + done) % share
            take = min(share - offset, size - done)
            pieces.append(self.full[index, offset : offset + take, :])
            done += take
        return jnp.concatenate(pieces, axis=0)

    def finish(self):
        for copy in self.copies + self.later:
            copy.wait_send()


def kernel(n_dp, n_tp, x_hbm, g_hbm, gate_hbm, up_hbm, w_hbm, warm_hbm, left_out, right_out,
           x_ref, gate_ref, up_ref, warm_ref, load_sems, wbuf, wsend, wrecv, gfull, gsend, grecv, hg, gate_slope, up_slope, gate_grad, up_grad, hidden,
           gram_own, gram_come, gram_sems, *exchange_refs):
    d, z = lax.axis_index("dp"), lax.axis_index("tensor")
    tokens = x_ref.shape[0]
    rank = warm_ref.shape[1]
    weight_columns = w_hbm.shape[1]
    per = n_dp // n_tp
    halves = wsend.shape[1]
    width = weight_columns // halves
    bits = n_dp.bit_length() - 1

    barrier = pltpu.get_barrier_semaphore()
    for step in range(1, n_dp):
        pl.semaphore_signal(barrier, inc=1, device_id={"dp": lax.rem(d + step, n_dp)}, device_id_type=MESH)
    for step in range(1, n_tp):
        pl.semaphore_signal(barrier, inc=1, device_id={"tensor": lax.rem(z + step, n_tp)}, device_id_type=MESH)

    loads = []

    def load(source, target):
        copy = pltpu.make_async_copy(source, target, load_sems.at[len(loads)])
        copy.start()
        loads.append(copy)
        return copy

    load_g = [
        load(g_hbm.at[:, pl.ds(part * weight_columns, weight_columns)], gfull.at[z * per + part])
        for part in range(per)
    ]
    load_w = [
        load(w_hbm.at[:, pl.ds(half * width, width)], wbuf.at[d, :, pl.ds(half * width, width)])
        for half in range(halves)
    ]
    load_warm, load_x = load(warm_hbm, warm_ref), load(x_hbm, x_ref)
    load_gate, load_up = load(gate_hbm, gate_ref), load(up_hbm, up_ref)
    for copy in load_g:
        copy.wait()
    pl.semaphore_wait(barrier, n_dp - 1 + n_tp - 1)

    def line_copy(way, hop, part, source, target):
        place = gfull.at[source * per + part]
        return pltpu.make_async_remote_copy(
            src_ref=place, dst_ref=place,
            send_sem=gsend.at[way, hop, part], recv_sem=grecv.at[way, hop, part],
            device_id={"tensor": target}, device_id_type=MESH,
        )

    def line_out(way, hop, part):
        if way == 0:
            return line_copy(way, hop, part, z - hop, z + 1)
        return line_copy(way, hop, part, z + hop, z - 1)

    def line_sends(way, hop):
        if way == 0:
            return jnp.logical_and(z - hop >= 0, z < n_tp - 1)
        return jnp.logical_and(z + hop <= n_tp - 1, z > 0)

    def line_start(hop, part):
        for way in (0, 1):
            @pl.when(line_sends(way, hop))
            def _():
                line_out(way, hop, part).start()

    def line_wait(hop, part):
        for way in (0, 1):
            source = z - 1 - hop if way == 0 else z + 1 + hop
            @pl.when(source >= 0 if way == 0 else source <= n_tp - 1)
            def _():
                line_copy(way, hop, part, source, z - 1 if way == 0 else z + 1).wait_recv()

    orders = [list(range(1, bits)) + [0], list(range(bits - 1, 0, -1)) + [0]]
    weight_copies = []

    def weight_copy(slot, half, partner, sem_slot):
        place = wbuf.at[flipped(d, slot), :, pl.ds(half * width, width)]
        return pltpu.make_async_remote_copy(
            src_ref=place, dst_ref=place,
            send_sem=wsend.at[sem_slot, half], recv_sem=wrecv.at[sem_slot, half],
            device_id={"dp": flipped(d, partner)}, device_id_type=MESH,
        )

    def weight_send(slot, half, first):
        for bit in orders[half][first:]:
            copy = weight_copy(slot, half, 1 << bit, slot ^ (1 << bit))
            copy.start()
            weight_copies.append(copy)

    def weight_wave(position):
        for index in range(1 << position):
            for half in range(halves):
                order = orders[half]
                slot = 1 << order[position]
                for place in range(position):
                    if index & (1 << place):
                        slot |= 1 << order[place]
                weight_copy(slot, half, 1 << order[position], slot).wait_recv()
                weight_send(slot, half, position + 1)

    gram_copies = []

    def finish():
        for exchange in exchanges:
            exchange.finish()
        for copy in gram_copies + weight_copies:
            copy.wait_send()
        for hop in range(n_tp - 1):
            for way in (0, 1):
                @pl.when(line_sends(way, hop))
                def _():
                    for part in range(per):
                        line_out(way, hop, part).wait_send()

    for part in range(per):
        line_start(0, part)
    for half in range(halves):
        load_w[half].wait()
        weight_send(0, half, 0)

    total_p, left_pair, left_last, mid_pair, mid_last, right_pair, right_last = exchanges = [
        Exchange(axis, count, exchange_refs[4 * index : 4 * index + 4])
        for index, (axis, count) in enumerate(
            [("tensor", n_tp)] + [("dp", n_dp)] * 2 + [("tensor", n_tp)] * 2 + [("dp", n_dp)] * 2
        )
    ]
    lefts = (gate_grad, up_grad, hidden)

    def right(k):
        if k < 2:
            return x_ref[...]
        return jnp.concatenate([gfull[z * per + part] for part in range(per)], axis=1)

    load_warm.wait()
    load_x.wait()
    for k in range(3):
        total_p.store(k * rank, exact_dot(warm_ref[k], right(k), NT))
    total_p.scatter()

    load_gate.wait()
    load_up.wait()
    gate = gate_ref[...].astype(F32)
    up = up_ref[...].astype(F32)
    sigma = 1.0 / (1.0 + jnp.exp(-gate))
    hidden[...] = (gate * sigma * up).astype(BF16)
    gate_slope[...] = up * sigma * (1.0 + gate * (1.0 - sigma))
    up_slope[...] = gate * sigma

    def product(source, parts):
        total = None
        for part in parts:
            block = source * per + part
            term = lax.dot_general(gfull[block], wbuf[block], NT, preferred_element_type=F32)
            total = term if total is None else total + term
        return total

    def line_use(hop, parts):
        for way in (0, 1):
            source = z - 1 - hop if way == 0 else z + 1 + hop
            @pl.when(source >= 0 if way == 0 else source <= n_tp - 1)
            def _():
                hg[...] += product(source, parts)

    last = n_tp - 2
    waves = list(range(bits - 1))
    for hop in range(last):
        for part in range(per):
            line_wait(hop, part)
            line_start(hop + 1, part)
            if part == per - 1 and waves:
                weight_wave(waves.pop(0))
        if hop == 0:
            total_p.gather()
    for position in waves:
        weight_wave(position)
    total_p.wait()

    def left_part(k):
        return exact_dot(total_p.load(k * rank, rank), lefts[k][...], NN) * (1.0 / tokens)

    left_last.store(0, left_part(2))
    left_last.scatter()
    weight_wave(bits - 1)
    hg[...] = product(z, range(per))
    for hop in range(last):
        line_use(hop, range(per))
    left_last.gather()
    for part in range(per):
        line_wait(last, part)
        line_use(last, [part])

    hidden_grad = hg[...]
    gate_grad[...] = (hidden_grad * gate_slope[...]).astype(BF16)
    up_grad[...] = (hidden_grad * up_slope[...]).astype(BF16)

    for k in range(2):
        left_pair.store(k * rank, left_part(k))
    left_pair.scatter()

    left_last.wait()
    mid_last.store(0, exact_dot(left_last.load(0, rank), hidden[...], NT))
    mid_last.scatter()
    left_pair.gather()
    mid_last.gather()
    left_pair.wait()
    raws = [left_pair.load(0, rank), left_pair.load(rank, rank), left_last.load(0, rank)]
    for k in range(2):
        mid_pair.store(k * rank, exact_dot(raws[k], lefts[k][...], NT))
    mid_pair.scatter()
    gram_own[...] = jnp.zeros_like(gram_own)
    for k in range(3):
        gram_own[:, k * rank : (k + 1) * rank] = lax.dot_general(
            raws[k], raws[k], NT, precision=HIGH, preferred_element_type=F32
        )
    for step in range(1, n_tp):
        copy = pltpu.make_async_remote_copy(
            src_ref=gram_own, dst_ref=gram_come.at[step - 1],
            send_sem=gram_sems.at[0, step - 1], recv_sem=gram_sems.at[1, step - 1],
            device_id={"tensor": lax.rem(z + step, n_tp)}, device_id_type=MESH,
        )
        copy.start()
        gram_copies.append(copy)

    mid_last.wait()
    right_last.store(0, exact_dot(mid_last.load(0, rank), right(2), NN))
    right_last.scatter()
    mid_pair.gather()
    right_last.gather()
    gram = gram_own[:, : 3 * rank]
    for step in range(1, n_tp):
        gram_copies[step - 1].wait_recv()
        gram = gram + gram_come[step - 1, :, : 3 * rank]
    cholesky = InverseCholesky(
        jnp.stack([gram[:, k * rank : (k + 1) * rank] for k in range(3)])
    )
    cholesky.run(0, rank // 4)
    mid_pair.wait()
    for k in range(2):
        right_pair.store(k * rank, exact_dot(mid_pair.load(k * rank, rank), right(k), NN))
    right_pair.scatter()

    cholesky.run(rank // 4, 3 * rank // 4)
    right_pair.gather()
    cholesky.run(3 * rank // 4, rank)
    inverse = cholesky.result()

    def orthogonal(k, raw):
        return lax.dot_general(inverse[k], raw, NN, precision=HIGH, preferred_element_type=F32)

    for k in range(3):
        left_out[k] = orthogonal(k, raws[k])
    right_last.wait()
    right_out[2] = orthogonal(2, right_last.load(0, rank)) * (1.0 / (tokens * n_dp))
    right_pair.wait()
    for k in range(2):
        right_out[k] = orthogonal(k, right_pair.load(k * rank, rank)) * (1.0 / (tokens * n_dp))

    finish()


def exchange_scratch(count, rows, width):
    share = rows // count
    return [
        pltpu.VMEM((count, share, width), F32),
        pltpu.VMEM((count - 1, share, width), F32),
        pltpu.VMEM((count, share, width), F32),
        pltpu.SemaphoreType.DMA((4, count - 1)),
    ]


def shards(n_dp, n_tp, inputs, grad_out, gate_pre, up_pre, down_weight, warm_start):
    tokens, own = inputs.shape
    hidden_units, weight_columns = down_weight.shape
    count, _, rank = warm_start.shape
    halves = 2 if weight_columns % 256 == 0 else 1
    vmem = pl.BlockSpec(memory_space=pltpu.VMEM)
    gram_width = pl.cdiv(count * rank, 128) * 128
    loads = 4 + halves + n_dp // n_tp
    left, right = pl.pallas_call(
        functools.partial(kernel, n_dp, n_tp),
        out_shape=(
            jax.ShapeDtypeStruct((count, rank, hidden_units), F32),
            jax.ShapeDtypeStruct((count, rank, own), F32),
        ),
        in_specs=[pl.BlockSpec(memory_space=pl.ANY)] * 6,
        out_specs=(vmem, vmem),
        scratch_shapes=[
            pltpu.VMEM(inputs.shape, BF16),
            pltpu.VMEM(gate_pre.shape, BF16),
            pltpu.VMEM(up_pre.shape, BF16),
            pltpu.VMEM((count, rank, own), F32),
            pltpu.SemaphoreType.DMA((loads,)),
            pltpu.VMEM((n_dp, hidden_units, weight_columns), BF16),
            pltpu.SemaphoreType.DMA((n_dp, halves)),
            pltpu.SemaphoreType.DMA((n_dp, halves)),
            pltpu.VMEM((n_dp, tokens, weight_columns), BF16),
            pltpu.SemaphoreType.DMA((2, n_tp - 1, n_dp // n_tp)),
            pltpu.SemaphoreType.DMA((2, n_tp - 1, n_dp // n_tp)),
            pltpu.VMEM((tokens, hidden_units), F32),
            pltpu.VMEM((tokens, hidden_units), F32),
            pltpu.VMEM((tokens, hidden_units), F32),
            pltpu.VMEM((tokens, hidden_units), BF16),
            pltpu.VMEM((tokens, hidden_units), BF16),
            pltpu.VMEM((tokens, hidden_units), BF16),
            pltpu.VMEM((rank, gram_width), F32),
            pltpu.VMEM((n_tp - 1, rank, gram_width), F32),
            pltpu.SemaphoreType.DMA((2, n_tp - 1)),
            *exchange_scratch(n_tp, 3 * rank, tokens),
            *exchange_scratch(n_dp, 2 * rank, hidden_units),
            *exchange_scratch(n_dp, rank, hidden_units),
            *exchange_scratch(n_tp, 2 * rank, tokens),
            *exchange_scratch(n_tp, rank, tokens),
            *exchange_scratch(n_dp, 2 * rank, own),
            *exchange_scratch(n_dp, rank, own),
        ],
        compiler_params=pltpu.CompilerParams(
            collective_id=0, has_side_effects=True, vmem_limit_bytes=56 * 1024 * 1024
        ),
        name="powersgd",
    )(inputs, grad_out, gate_pre, up_pre, down_weight, jnp.swapaxes(warm_start, 1, 2))
    return jnp.swapaxes(left, 1, 2), jnp.swapaxes(right, 1, 2)


def solution(mesh):
    placed = (
        P("dp", "tensor"),
        P("dp", "tensor"),
        P("dp", "tensor"),
        P("dp", "tensor"),
        P("tensor", "dp"),
        P(None, "tensor", None),
    )
    return jax.shard_map(
        functools.partial(shards, mesh.shape["dp"], mesh.shape["tensor"]),
        mesh=mesh,
        in_specs=placed,
        out_specs=(P(None, "tensor", None), P(None, "tensor", None)),
        check_vma=False,
    )
```
